32 devices in a mesh: dp: 8 (over z, y), tensor: 4 (over x, core).
Axes of the slice: x: 2, y: 2, z: 4, core: 2. Of those that a mesh axis runs over, the one named last changes fastest.
Arguments:
- prompt_hidden: bfloat16 [1024, 5120], P('dp'), may hold values from -6 to 6
- w_key: bfloat16 [5120, 1024], P(None, 'tensor'), may hold values from -0.078125 to 0.078125
- w_value: bfloat16 [5120, 1024], P(None, 'tensor'), may hold values from -0.078125 to 0.078125
- resp_query: bfloat16 [1024, 8192], P('dp', 'tensor'), may hold values from -160 to 160
- resp_kv: bfloat16 [2, 1024, 1024], P(None, 'dp', 'tensor'), may hold values from -6 to 6
- cotangent: bfloat16 [1024, 8192], P('dp', 'tensor'), may hold values from -6 to 6
- prompt_len: int32 [8], replicated, may hold values from 32 to 128, as said below
- resp_len: int32 [8], P('dp'), may hold values from 16 to 128, as said below
- offsets: int32 [8], P('dp'), may hold values from 0 to 3, as said below
- advantage: int32 [8], P('dp'), may hold values from -2 to 2
Outputs:
- attn_out: bfloat16 [1024, 8192], P('dp', 'tensor')
- grad_query: bfloat16 [1024, 8192], P('dp', 'tensor')
- grad_resp_kv: bfloat16 [2, 1024, 1024], P(None, 'dp', 'tensor')
- grad_prompt_hidden: bfloat16 [1024, 5120], P('dp', 'tensor')
The draws below stay inside these ranges and needn't reach their ends.
Inputs may be any that keep to these rules, and one draw needn't show every extreme that they name: `prompt_len`: some prompt has exactly 128 tokens. `resp_len`: some slot's response has exactly 128 tokens. `offsets`: some slot has offset 0 and some slot offset 4 - 1.
All inputs are finite; a program needn't handle non-finite values.
Results may differ from the reference program's by a relative error of at most 0.012.
Values may be sent and summed in bfloat16 or wider, within the bound.
A program may use at most 64 MiB of HBM per device.

```python
import jax
import jax.numpy as jnp
from jax import lax

D = 5120
HD = 128
QHEADS = 64
KVHEADS = 8
PLEN = 128
RLEN = 128
S_DEV = 1
WIN = 4
PROMPTS = 8
SLOTS = 8
RESP_ROWS = 1024
PROMPT_ROWS = 1024
N_TENSOR = 4


def base_keys(key):
    raw = jax.random.normal(key, (RESP_ROWS, KVHEADS, HD), jnp.float32)
    return jnp.clip(raw, -5.0, 5.0)


def draw_resp_kv(key, part):
    keys = base_keys(key)
    key = jax.random.fold_in(key, 3)
    values = jnp.clip(jax.random.normal(key, keys.shape, jnp.float32), -5.0, 5.0)
    return jnp.stack([keys, values]).reshape(2, RESP_ROWS, KVHEADS * HD).astype(jnp.bfloat16)


def draw_resp_query(key, part):
    key = jax.random.fold_in(key, 5)
    values = jnp.clip(jax.random.normal(key, (RESP_ROWS, QHEADS, HD), jnp.float32), -5.0, 5.0)
    return values.reshape(RESP_ROWS, QHEADS * HD).astype(jnp.bfloat16)


def draw_prompt_len(key, part):
    key = jax.random.fold_in(key, 7)
    values = jax.random.randint(key, (PROMPTS,), PLEN // 4, PLEN + 1)
    spot = jax.random.randint(jax.random.fold_in(key, 1), (), 0, PROMPTS)
    return jnp.where(jnp.arange(PROMPTS) == spot, PLEN, values).astype(jnp.int32)


def draw_resp_len(key, part):
    key = jax.random.fold_in(key, 9)
    values = jax.random.randint(key, (SLOTS,), RLEN // 8, RLEN + 1)
    spot = jax.random.randint(jax.random.fold_in(key, 1), (), 0, SLOTS)
    return jnp.where(jnp.arange(SLOTS) == spot, RLEN, values).astype(jnp.int32)


def draw_offsets(key, part):
    key = jax.random.fold_in(key, 13)
    values = jax.random.randint(key, (SLOTS,), 0, WIN)
    spot = jax.random.randint(jax.random.fold_in(key, 1), (), 0, SLOTS)
    other = (spot + 1 + jax.random.randint(jax.random.fold_in(key, 2), (), 0, SLOTS - 1)) % SLOTS
    index = jnp.arange(SLOTS)
    values = jnp.where(index == spot, WIN - 1, values)
    return jnp.where(index == other, 0, values).astype(jnp.int32)


def with_ends(entries, key, least, high):
    shape = entries.shape
    index_at = [jax.random.randint(jax.random.fold_in(key, axis), (), 0, shape[axis]) for axis in range(len(shape))]
    entries = entries.at[tuple(index_at)].set(least)
    longest = shape.index(max(shape))
    index_at[longest] = (index_at[longest] + 1) % shape[longest]
    return entries.at[tuple(index_at)].set(high)


def levels(key, shape, pieces, least, high):
    factor_of = 1.0
    for axis_at, blocks in pieces:
        draws = jax.random.uniform(jax.random.fold_in(jax.random.fold_in(key, 6), axis_at), (blocks,), jnp.float32, least / len(pieces), high / len(pieces))
        factor_of = factor_of * jnp.repeat(jnp.exp(draws), shape[axis_at] // blocks).reshape((-1,) + (1,) * (len(shape) - 1 - axis_at))
    return factor_of


def scatter_about(rng, extent, deviation, most, shards=(), kind=jnp.bfloat16):
    result = jax.random.normal(rng, extent, jnp.float32) * deviation
    if len(shards) > 0:
        result = levels(rng, extent, shards, -0.22, 0.18) * result
    return jnp.clip(result, min=-most, max=most).astype(kind)


def setup_inputs(seed: int = 0) -> dict:
    key_of = jax.random.split(jax.random.key(seed), 11)
    prompt_hidden = scatter_about(key_of[0], (PROMPT_ROWS, D), 1.0, 6.0, ((0, 8),))
    w_key = scatter_about(key_of[1], (D, KVHEADS * HD), D ** -0.5, 0.078125, ((1, 4),))
    w_value = scatter_about(key_of[2], (D, KVHEADS * HD), D ** -0.5, 0.078125, ((1, 4),))
    resp_query = draw_resp_query(jax.random.fold_in(key_of[10], 71), 0)
    resp_kv = draw_resp_kv(jax.random.fold_in(key_of[10], 71), 0)
    cotangent = scatter_about(key_of[5], (RESP_ROWS, QHEADS * HD), 1.0, 6.0, ((0, 8), (1, 4)))
    prompt_len = draw_prompt_len(jax.random.fold_in(key_of[10], 71), 0)
    resp_len = draw_resp_len(jax.random.fold_in(key_of[10], 71), 0)
    offsets = draw_offsets(jax.random.fold_in(key_of[10], 71), 0)
    advantage = with_ends(jax.random.randint(key_of[9], (SLOTS,), -2, 3), jax.random.fold_in(key_of[9], 1), -2, 2).astype(jnp.int32)
    return dict(prompt_hidden=prompt_hidden, w_key=w_key, w_value=w_value, resp_query=resp_query, resp_kv=resp_kv, cotangent=cotangent, prompt_len=prompt_len, resp_len=resp_len, offsets=offsets, advantage=advantage)


MASKED_SCORE = -1e30


def rounded(values):
    return lax.optimization_barrier(values.astype(jnp.bfloat16)).astype(jnp.float32)


def slot_terms(queries, own_keys, own_values, prompt_keys, prompt_values, resp_length, prompt_length, grad_out):
    slot_rows = queries.shape[0]
    prefix_rows = prompt_keys.shape[0]
    score_scale = HD ** -0.5
    position = jnp.arange(slot_rows)
    row_valid = (position < resp_length).astype(jnp.float32)[:, None, None, None]
    causal = (position[:, None] >= position[None, :])[:, None, None, :]
    prefix_ok = (jnp.arange(prefix_rows) < prompt_length)[None, None, None, :]
    pre_scores = jnp.einsum("rkgd,pkd->rkgp", queries, prompt_keys) * score_scale
    pre_scores = jnp.where(prefix_ok, pre_scores, MASKED_SCORE)
    own_scores = jnp.einsum("rkgd,ukd->rkgu", queries, own_keys) * score_scale
    own_scores = jnp.where(causal, own_scores, MASKED_SCORE)
    top = jnp.maximum(pre_scores.max(-1), own_scores.max(-1))
    summed = jnp.sum(jnp.exp(pre_scores - top[..., None]), -1) + jnp.sum(jnp.exp(own_scores - top[..., None]), -1)
    log_total = top + jnp.log(summed)
    pre_probs = jnp.exp(pre_scores - log_total[..., None])
    own_probs = jnp.exp(own_scores - log_total[..., None])
    pre_weights = rounded(pre_probs)
    own_weights = rounded(own_probs)
    output = jnp.einsum("rkgp,pkd->rkgd", pre_weights, prompt_values) + jnp.einsum("rkgu,ukd->rkgd", own_weights, own_values)
    output = output * row_valid
    grad_out = grad_out * row_valid
    grad_pre = jnp.einsum("rkgd,pkd->rkgp", grad_out, prompt_values)
    grad_own = jnp.einsum("rkgd,ukd->rkgu", grad_out, own_values)
    row_delta = jnp.sum(grad_out * output, -1)
    pre_dscores = rounded(pre_probs * (grad_pre - row_delta[..., None]))
    own_dscores = rounded(own_probs * (grad_own - row_delta[..., None]))
    grad_queries = (jnp.einsum("rkgp,pkd->rkgd", pre_dscores, prompt_keys) + jnp.einsum("rkgu,ukd->rkgd", own_dscores, own_keys)) * score_scale
    grad_key_own = jnp.einsum("rkgu,rkgd->ukd", own_dscores, queries) * score_scale
    grad_value_own = jnp.einsum("rkgu,rkgd->ukd", own_weights, grad_out)
    grad_key_pre = jnp.einsum("rkgp,rkgd->pkd", pre_dscores, queries) * score_scale
    grad_value_pre = jnp.einsum("rkgp,rkgd->pkd", pre_weights, grad_out)
    return (output.astype(jnp.bfloat16), grad_queries.astype(jnp.bfloat16), grad_key_own.astype(jnp.bfloat16),
            grad_value_own.astype(jnp.bfloat16), grad_key_pre, grad_value_pre)


def reference(prompt_hidden, w_key, w_value, resp_query, resp_kv, cotangent, prompt_len, resp_len, offsets, advantage):
    group_size = QHEADS // KVHEADS
    keys_all = jnp.dot(prompt_hidden, w_key, preferred_element_type=jnp.float32).astype(jnp.bfloat16)
    values_all = jnp.dot(prompt_hidden, w_value, preferred_element_type=jnp.float32).astype(jnp.bfloat16)
    keys_all = keys_all.reshape(PROMPTS, PLEN, KVHEADS, HD)
    values_all = values_all.reshape(PROMPTS, PLEN, KVHEADS, HD)
    query_slots = resp_query.reshape(SLOTS, RLEN, KVHEADS, group_size, HD)
    cot_slots = cotangent.reshape(SLOTS, RLEN, KVHEADS, group_size, HD)
    own_key_slots = resp_kv[0].reshape(SLOTS, RLEN, KVHEADS, HD)
    own_value_slots = resp_kv[1].reshape(SLOTS, RLEN, KVHEADS, HD)
    slot_ids = jnp.arange(SLOTS, dtype=jnp.int32)
    owner_rank = ((slot_ids // S_DEV - offsets) % PROMPTS).astype(jnp.int32)

    def step(prompt_grads, slot_index):
        prompt_index = owner_rank[slot_index]
        prompt_keys = lax.dynamic_index_in_dim(keys_all, prompt_index, 0, keepdims=False).astype(jnp.float32)
        prompt_values = lax.dynamic_index_in_dim(values_all, prompt_index, 0, keepdims=False).astype(jnp.float32)
        queries = lax.dynamic_index_in_dim(query_slots, slot_index, 0, keepdims=False).astype(jnp.float32)
        own_keys = lax.dynamic_index_in_dim(own_key_slots, slot_index, 0, keepdims=False).astype(jnp.float32)
        own_values = lax.dynamic_index_in_dim(own_value_slots, slot_index, 0, keepdims=False).astype(jnp.float32)
        factor = advantage[slot_index].astype(jnp.float32)
        grad_out = lax.dynamic_index_in_dim(cot_slots, slot_index, 0, keepdims=False).astype(jnp.float32) * factor
        results = slot_terms(queries, own_keys, own_values, prompt_keys, prompt_values,
                             resp_len[slot_index], prompt_len[prompt_index], grad_out)
        prompt_grads = prompt_grads.at[prompt_index].add(jnp.stack([results[4], results[5]]))
        return prompt_grads, results[:4]

    start = jnp.zeros((PROMPTS, 2, PLEN, KVHEADS, HD), jnp.float32)
    prompt_grads, outputs = lax.scan(step, start, slot_ids)
    attn_out = outputs[0].reshape(RESP_ROWS, QHEADS * HD)
    grad_query = outputs[1].reshape(RESP_ROWS, QHEADS * HD)
    grad_resp_kv = jnp.stack([outputs[2].reshape(RESP_ROWS, KVHEADS * HD), outputs[3].reshape(RESP_ROWS, KVHEADS * HD)])
    rounded_grads = prompt_grads.astype(jnp.bfloat16).reshape(PROMPTS, 2, PLEN, KVHEADS * HD)
    group_width = (KVHEADS // N_TENSOR) * HD
    summed = jnp.zeros((PROMPT_ROWS, D), jnp.float32)
    for group in range(N_TENSOR):
        lower = group * group_width
        key_part = rounded_grads[:, 0, :, lower:lower + group_width].reshape(PROMPT_ROWS, group_width)
        value_part = rounded_grads[:, 1, :, lower:lower + group_width].reshape(PROMPT_ROWS, group_width)
        partial_sum = jnp.dot(key_part, w_key[:, lower:lower + group_width].T, preferred_element_type=jnp.float32)
        partial_sum = partial_sum + jnp.dot(value_part, w_value[:, lower:lower + group_width].T, preferred_element_type=jnp.float32)
        summed = summed + rounded(partial_sum)
    return attn_out, grad_query, grad_resp_kv, summed.astype(jnp.bfloat16)
```

```python
import functools

import jax
import jax.numpy as jnp
from jax import lax
from jax.experimental import pallas as pl
from jax.experimental.pallas import tpu as pltpu
from jax.sharding import PartitionSpec as P

HD = 128
MASKED_SCORE = -1e30
PAIR = 2
PROJ_CHUNKS = 4
COL_CHUNKS = 5
MESH = pl.DeviceIdType.MESH
NT = (((1,), (1,)), ((), ()))
TN = (((0,), (0,)), ((), ()))


def dot_nt(a, b):
    return lax.dot_general(a, b, NT, preferred_element_type=jnp.float32)


def dot_tn(a, b):
    return lax.dot_general(a, b, TN, preferred_element_type=jnp.float32)


def dot_nn(a, b):
    return jnp.dot(a, b, preferred_element_type=jnp.float32)


def kernel(
    n_dp, n_tensor, window,
    hid_hbm, wk_hbm, wv_hbm, q_hbm, okv_hbm, cot_hbm, plen, rlen, offs, adv,
    attn_hbm, gq_hbm, gkv_hbm, gph_hbm,
    hid, wk, wv, q, cot, okv, fk, fv, e_own, gp_own, gs, m_own, l_own, d_own,
    p_pre, ds_pre, p_own, ds_own, ratio, delta_s,
    tx, mine, rx, attn, gq, gkv, gph, sib_tx, sib_rx, x_tx, x_rx, near,
    in_sem, out_sem, fo_send, fo_recv, fi_send, fi_recv, sib_send, sib_recv, x_send, x_recv,
):
    me = lax.axis_index("dp")
    t_me = lax.axis_index("tensor")
    n_x = n_tensor // 2
    x_me, core = lax.div(t_me, 2), lax.rem(t_me, 2)
    sibling = x_me * 2 + 1 - core
    rows, width = q.shape
    prefix_rows, depth = hid.shape
    kv_width = wk.shape[1]
    kv_heads = kv_width // HD
    pairs = width // HD // PAIR
    group_pairs = pairs // kv_heads
    scale = HD ** (-0.5)
    far = range(window - 1, 0, -1)

    def ahead(d):
        return (lax.rem(me + d, n_dp), t_me)

    def behind(d):
        return (lax.rem(me + n_dp - d, n_dp), t_me)

    def across(dx):
        return (me, lax.rem(x_me + dx, n_x) * 2 + core)

    barrier = pltpu.get_barrier_semaphore()
    partners = [ahead(d) for d in far] + [behind(d) for d in far]
    partners += [(me, sibling)] + [across(dx) for dx in range(1, n_x)]
    for partner in partners:
        pl.semaphore_signal(barrier, inc=1, device_id=partner, device_id_type=MESH)

    step = depth // PROJ_CHUNKS
    loads = {}

    def load(name, src, dst):
        copy = pltpu.make_async_copy(src, dst, in_sem.at[len(loads)])
        copy.start()
        loads[name] = copy

    for c in range(PROJ_CHUNKS):
        part = pl.ds(c * step, step)
        load(("h", c), hid_hbm.at[:, part], hid.at[:, part])
        load(("k", c), wk_hbm.at[part, :], wk.at[part, :])
    for c in range(PROJ_CHUNKS):
        part = pl.ds(c * step, step)
        load(("v", c), wv_hbm.at[part, :], wv.at[part, :])
    load("okv", okv_hbm, okv)
    load("q", q_hbm, q)
    load("cot", cot_hbm, cot)

    def projected(name, weight):
        total = None
        for c in range(PROJ_CHUNKS):
            if name == "k":
                loads[("h", c)].wait()
            loads[(name, c)].wait()
            part = pl.ds(c * step, step)
            term = dot_nn(hid[:, part], weight[part, :])
            total = term if total is None else total + term
        return total.astype(jnp.bfloat16)

    def send(src, dst, send_sem, recv_sem, device):
        copy = pltpu.make_async_remote_copy(
            src_ref=src, dst_ref=dst, send_sem=send_sem, recv_sem=recv_sem,
            device_id=device, device_id_type=MESH,
        )
        copy.start()
        return copy

    out_key = []
    out_value = []
    fk[0] = projected("k", wk)
    pl.semaphore_wait(barrier, len(partners))
    for d in far:
        out_key.append(send(fk.at[0], fk.at[d], fo_send.at[0, d], fo_recv.at[0, d], ahead(d)))
    fv[0] = projected("v", wv)
    for d in far:
        out_value.append(send(fv.at[0], fv.at[d], fo_send.at[1, d], fo_recv.at[1, d], ahead(d)))

    off = offs[0]
    owner = lax.rem(me - off + n_dp, n_dp)
    chosen_len = plen[owner]
    row_at = lax.broadcasted_iota(jnp.int32, (PAIR * rows, rows), 0)
    row_at = jnp.where(row_at >= rows, row_at - rows, row_at)
    key_at = lax.broadcasted_iota(jnp.int32, (PAIR * rows, rows), 1)
    causal = row_at >= key_at
    valid = jnp.where(row_at[:, :1] < rlen[0], 1.0, 0.0)
    factor = valid * adv[0].astype(jnp.float32)
    prefix_ok = lax.broadcasted_iota(jnp.int32, (PAIR * rows, prefix_rows), 1) < chosen_len

    def head_cols(ref, p):
        return jnp.concatenate(
            [ref[:, (p * PAIR + u) * HD:(p * PAIR + u + 1) * HD] for u in range(PAIR)], axis=0
        )

    def put_cols(ref, p, value):
        for u in range(PAIR):
            ref[:, (p * PAIR + u) * HD:(p * PAIR + u + 1) * HD] = value[u * rows:(u + 1) * rows]

    def cols(g):
        return slice(g * HD, (g + 1) * HD)

    for name in ("okv", "q", "cot"):
        loads[name].wait()
    for p in range(pairs):
        g = p // group_pairs
        s = dot_nt(head_cols(q, p), okv[0, :, cols(g)]) * scale
        s = jnp.where(causal, s, MASKED_SCORE)
        m = jnp.max(s, axis=1, keepdims=True)
        e = jnp.exp(s - m)
        grad = (head_cols(cot, p).astype(jnp.float32) * factor).astype(jnp.bfloat16)
        gp = dot_nt(grad, okv[1, :, cols(g)])
        gs[p] = grad
        e_own[p] = e
        gp_own[p] = gp
        m_own[p] = m
        l_own[p] = jnp.sum(e, axis=1, keepdims=True)
        d_own[p] = jnp.sum(e * gp, axis=1, keepdims=True)

    for copy in out_key + out_value:
        copy.wait_recv()
    back = []
    for g in range(kv_heads):
        keys = fk[off, :, cols(g)]
        values = fv[off, :, cols(g)]
        mine_pairs = range(g * group_pairs, (g + 1) * group_pairs)
        for p in mine_pairs:
            s = dot_nt(head_cols(q, p), keys) * scale
            s = jnp.where(prefix_ok, s, MASKED_SCORE)
            m = jnp.maximum(jnp.max(s, axis=1, keepdims=True), m_own[p])
            e = jnp.exp(s - m)
            a = jnp.exp(m_own[p] - m)
            r = 1.0 / (a * l_own[p] + jnp.sum(e, axis=1, keepdims=True))
            probs = e * r
            gp = dot_nt(gs[p], values)
            a = a * r
            delta = jnp.sum(probs * gp, axis=1, keepdims=True) + a * d_own[p]
            p_pre[p] = probs.astype(jnp.bfloat16)
            ds_pre[p] = (probs * (gp - delta)).astype(jnp.bfloat16)
            ratio[p] = a
            delta_s[p] = delta
        q_all = jnp.concatenate([head_cols(q, p) for p in mine_pairs], axis=0)
        ds_all = jnp.concatenate([ds_pre[p] for p in mine_pairs], axis=0)
        p_all = jnp.concatenate([p_pre[p] for p in mine_pairs], axis=0)
        g_all = jnp.concatenate([gs[p] for p in mine_pairs], axis=0)
        both = [dot_tn(ds_all, q_all) * scale, dot_tn(p_all, g_all)]
        for i in range(2):
            for d in range(window):
                share = both[i] * jnp.where(off == d, 1.0, 0.0)
                if d == 0:
                    mine[g, i] = share
                else:
                    tx[d, g, i] = share.astype(jnp.bfloat16)
        for d in far:
            back.append(
                send(tx.at[d, g], rx.at[d, g], fi_send.at[g, d], fi_recv.at[g, d], behind(d))
            )

    stores = []

    def store(src, dst):
        copy = pltpu.make_async_copy(src, dst, out_sem.at[len(stores)])
        copy.start()
        stores.append(copy)

    for g in range(kv_heads):
        mine_pairs = range(g * group_pairs, (g + 1) * group_pairs)
        keys = jnp.concatenate([fk[off, :, cols(g)], okv[0, :, cols(g)]], axis=0)
        values = jnp.concatenate([fv[off, :, cols(g)], okv[1, :, cols(g)]], axis=0)
        for p in mine_pairs:
            probs = e_own[p] * ratio[p]
            ds = (probs * (gp_own[p] - delta_s[p])).astype(jnp.bfloat16)
            probs = probs.astype(jnp.bfloat16)
            p_own[p] = probs
            ds_own[p] = ds
            out = dot_nn(jnp.concatenate([p_pre[p], probs], axis=1), values) * valid
            put_cols(attn, p, out.astype(jnp.bfloat16))
            grad = dot_nn(jnp.concatenate([ds_pre[p], ds], axis=1), keys) * scale
            put_cols(gq, p, grad.astype(jnp.bfloat16))
        q_all = jnp.concatenate([head_cols(q, p) for p in mine_pairs], axis=0)
        ds_all = jnp.concatenate([ds_own[p] for p in mine_pairs], axis=0)
        p_all = jnp.concatenate([p_own[p] for p in mine_pairs], axis=0)
        g_all = jnp.concatenate([gs[p] for p in mine_pairs], axis=0)
        gkv[0, :, cols(g)] = (dot_tn(ds_all, q_all) * scale).astype(jnp.bfloat16)
        gkv[1, :, cols(g)] = dot_tn(p_all, g_all).astype(jnp.bfloat16)
    store(attn, attn_hbm)
    store(gq, gq_hbm)
    store(gkv, gkv_hbm)

    for copy in back:
        copy.wait_recv()
    summed = [[], []]
    for g in range(kv_heads):
        for i in range(2):
            total = mine[g, i]
            for d in range(1, window):
                total = total + rx[d, g, i].astype(jnp.float32)
            summed[i].append(total.astype(jnp.bfloat16))
    key_grad = jnp.concatenate(summed[0], axis=1)
    value_grad = jnp.concatenate(summed[1], axis=1)
    block = depth // n_tensor
    chunk = block // COL_CHUNKS

    def partial(dx, to_core, c):
        at = (lax.rem(x_me + dx, n_x) * 2 + to_core) * block + c * chunk
        part = pl.ds(pl.multiple_of(at, chunk), chunk)
        return dot_nt(key_grad, wk[part, :]) + dot_nt(value_grad, wv[part, :])

    to_sibling = {}
    to_across = []
    for dx in list(range(1, n_x)) + [0]:
        for c in range(COL_CHUNKS):
            sib_tx[dx, c] = partial(dx, 1 - core, c).astype(jnp.bfloat16)
            to_sibling[dx, c] = send(
                sib_tx.at[dx, c], sib_rx.at[dx, c], sib_send.at[dx, c], sib_recv.at[dx, c],
                (me, sibling),
            )
        for c in range(COL_CHUNKS):
            own = partial(dx, core, c)
            to_sibling[dx, c].wait_recv()
            own = own + sib_rx[dx, c].astype(jnp.float32)
            if dx == 0:
                near[c] = own
            else:
                x_tx[dx, c] = own.astype(jnp.bfloat16)
                to_across.append(
                    send(
                        x_tx.at[dx, c], x_rx.at[dx, c], x_send.at[dx, c], x_recv.at[dx, c],
                        across(dx),
                    )
                )
    for c in range(COL_CHUNKS):
        own = near[c]
        for dx in range(1, n_x):
            to_across[(dx - 1) * COL_CHUNKS + c].wait_recv()
            own = own + x_rx[dx, c].astype(jnp.float32)
        gph[:, c * chunk:(c + 1) * chunk] = own.astype(jnp.bfloat16)
    store(gph, gph_hbm)
    for copy in out_key + out_value + back + list(to_sibling.values()) + to_across:
        copy.wait_send()
    for copy in stores:
        copy.wait()


def local(
    prompt_hidden, w_key, w_value, resp_query, resp_kv, cotangent,
    prompt_len, resp_len, offsets, advantage,
):
    n_dp, n_tensor = lax.axis_size("dp"), lax.axis_size("tensor")
    window = min(8, n_dp // 2)
    n_x = n_tensor // 2
    rows, width = resp_query.shape
    prefix_rows, depth = prompt_hidden.shape
    kv_width = w_key.shape[1]
    kv_heads = kv_width // HD
    pairs = width // HD // PAIR
    stacked = PAIR * rows
    block = depth // n_tensor
    chunk = block // COL_CHUNKS
    bf, f32 = jnp.bfloat16, jnp.float32
    vmem = pltpu.VMEM
    scratch = [
        vmem((prefix_rows, depth), bf),
        vmem((depth, kv_width), bf),
        vmem((depth, kv_width), bf),
        vmem((rows, width), bf),
        vmem((rows, width), bf),
        vmem((2, rows, kv_width), bf),
        vmem((window, prefix_rows, kv_width), bf),
        vmem((window, prefix_rows, kv_width), bf),
        vmem((pairs, stacked, rows), f32),
        vmem((pairs, stacked, rows), f32),
        vmem((pairs, stacked, HD), bf),
        vmem((pairs, stacked, 1), f32),
        vmem((pairs, stacked, 1), f32),
        vmem((pairs, stacked, 1), f32),
        vmem((pairs, stacked, prefix_rows), bf),
        vmem((pairs, stacked, prefix_rows), bf),
        vmem((pairs, stacked, rows), bf),
        vmem((pairs, stacked, rows), bf),
        vmem((pairs, stacked, 1), f32),
        vmem((pairs, stacked, 1), f32),
        vmem((window, kv_heads, 2, prefix_rows, HD), bf),
        vmem((kv_heads, 2, prefix_rows, HD), f32),
        vmem((window, kv_heads, 2, prefix_rows, HD), bf),
        vmem((rows, width), bf),
        vmem((rows, width), bf),
        vmem((2, rows, kv_width), bf),
        vmem((prefix_rows, block), bf),
        vmem((n_x, COL_CHUNKS, prefix_rows, chunk), bf),
        vmem((n_x, COL_CHUNKS, prefix_rows, chunk), bf),
        vmem((n_x, COL_CHUNKS, prefix_rows, chunk), bf),
        vmem((n_x, COL_CHUNKS, prefix_rows, chunk), bf),
        vmem((COL_CHUNKS, prefix_rows, chunk), f32),
        pltpu.SemaphoreType.DMA((3 * PROJ_CHUNKS + 3,)),
        pltpu.SemaphoreType.DMA((4,)),
        pltpu.SemaphoreType.DMA((2, window)),
        pltpu.SemaphoreType.DMA((2, window)),
        pltpu.SemaphoreType.DMA((kv_heads, window)),
        pltpu.SemaphoreType.DMA((kv_heads, window)),
        pltpu.SemaphoreType.DMA((n_x, COL_CHUNKS)),
        pltpu.SemaphoreType.DMA((n_x, COL_CHUNKS)),
        pltpu.SemaphoreType.DMA((n_x, COL_CHUNKS)),
        pltpu.SemaphoreType.DMA((n_x, COL_CHUNKS)),
    ]
    anywhere = pl.BlockSpec(memory_space=pl.ANY)
    scalars = pl.BlockSpec(memory_space=pltpu.SMEM)
    return pl.pallas_call(
        functools.partial(kernel, n_dp, n_tensor, window),
        out_shape=(
            jax.ShapeDtypeStruct((rows, width), bf),
            jax.ShapeDtypeStruct((rows, width), bf),
            jax.ShapeDtypeStruct((2, rows, kv_width), bf),
            jax.ShapeDtypeStruct((prefix_rows, block), bf),
        ),
        in_specs=[anywhere] * 6 + [scalars] * 4,
        out_specs=(anywhere,) * 4,
        scratch_shapes=scratch,
        compiler_params=pltpu.CompilerParams(
            collective_id=0, has_side_effects=True, vmem_limit_bytes=56 * 2**20
        ),
    )(
        prompt_hidden, w_key, w_value, resp_query, resp_kv, cotangent,
        prompt_len, resp_len, offsets, advantage,
    )


def solution(mesh):
    placed = (
        P("dp", None),
        P(None, "tensor"),
        P(None, "tensor"),
        P("dp", "tensor"),
        P(None, "dp", "tensor"),
        P("dp", "tensor"),
        P(),
        P("dp"),
        P("dp"),
        P("dp"),
    )
    return jax.shard_map(
        local,
        mesh=mesh,
        in_specs=placed,
        out_specs=(
            P("dp", "tensor"),
            P("dp", "tensor"),
            P(None, "dp", "tensor"),
            P("dp", "tensor"),
        ),
        check_vma=False,
    )
```

```python
import functools

import jax
import jax.numpy as jnp
from jax import lax
from jax.experimental import pallas as pl
from jax.experimental.pallas import tpu as pltpu
from jax.sharding import PartitionSpec as P

HD = 128
MASKED_SCORE = -1e30
PAIR = 2
PROJ_CHUNKS = 4
COL_CHUNKS = 5
PARTS = 2
MESH = pl.DeviceIdType.MESH
NT = (((1,), (1,)), ((), ()))
TN = (((0,), (0,)), ((), ()))


def dot_nt(a, b):
    return lax.dot_general(a, b, NT, preferred_element_type=jnp.float32)


def dot_tn(a, b):
    return lax.dot_general(a, b, TN, preferred_element_type=jnp.float32)


def dot_nn(a, b):
    return jnp.dot(a, b, preferred_element_type=jnp.float32)


def kernel(
    n_dp, n_tensor, window,
    hid_hbm, wk_hbm, wv_hbm, q_hbm, okv_hbm, cot_hbm, plen, rlen, offs, adv,
    attn_hbm, gq_hbm, gkv_hbm, gph_hbm,
    hid, wk, wv, q, cot, okv, kv, chosen, e_own, gp_own, gs, m_own, l_own, d_own,
    p_pre, ds_pre, p_own, ds_own, ratio, delta_s,
    tx, mine, rx, attn, gq, gkv, gph, sib_tx, sib_rx, x_tx, x_rx, near,
    in_sem, out_sem, fo_send, fo_recv, fi_send, fi_recv, sib_send, sib_recv, x_send, x_recv,
):
    me = lax.axis_index("dp")
    t_me = lax.axis_index("tensor")
    n_x = n_tensor // 2
    x_me, core = lax.div(t_me, 2), lax.rem(t_me, 2)
    sibling = x_me * 2 + 1 - core
    rows, width = q.shape
    prefix_rows, depth = hid.shape
    kv_width = wk.shape[1]
    kv_heads = kv_width // HD
    pairs = width // HD // PAIR
    group_pairs = pairs // kv_heads
    scale = HD ** (-0.5)
    far = range(window - 1, 0, -1)

    def ahead(d):
        return (lax.rem(me + d, n_dp), t_me)

    def behind(d):
        return (lax.rem(me + n_dp - d, n_dp), t_me)

    def across(dx):
        return (me, lax.rem(x_me + dx, n_x) * 2 + core)

    barrier = pltpu.get_barrier_semaphore()
    partners = [ahead(d) for d in far] + [behind(d) for d in far]
    partners += [(me, sibling)] + [across(dx) for dx in range(1, n_x)]
    for partner in partners:
        pl.semaphore_signal(barrier, inc=1, device_id=partner, device_id_type=MESH)

    step = depth // PROJ_CHUNKS
    loads = {}

    def load(name, src, dst):
        copy = pltpu.make_async_copy(src, dst, in_sem.at[len(loads)])
        copy.start()
        loads[name] = copy

    for c in range(PROJ_CHUNKS):
        part = pl.ds(c * step, step)
        load(("h", c), hid_hbm.at[:, part], hid.at[:, part])
        load(("k", c), wk_hbm.at[part, :], wk.at[part, :])
    for c in range(PROJ_CHUNKS):
        part = pl.ds(c * step, step)
        load(("v", c), wv_hbm.at[part, :], wv.at[part, :])
    load("okv", okv_hbm, okv)
    load("q", q_hbm, q)
    load("cot", cot_hbm, cot)

    def projected(name, weight):
        total = None
        for c in range(PROJ_CHUNKS):
            if name == "k":
                loads[("h", c)].wait()
            loads[(name, c)].wait()
            part = pl.ds(c * step, step)
            term = dot_nn(hid[:, part], weight[part, :])
            total = term if total is None else total + term
        return total.astype(jnp.bfloat16)

    def send(src, dst, send_sem, recv_sem, device):
        copy = pltpu.make_async_remote_copy(
            src_ref=src, dst_ref=dst, send_sem=send_sem, recv_sem=recv_sem,
            device_id=device, device_id_type=MESH,
        )
        copy.start()
        return copy

    for i, (name, weight) in enumerate((("k", wk), ("v", wv))):
        block = projected(name, weight)
        for g in range(kv_heads):
            kv[0, g, i] = block[:, g * HD:(g + 1) * HD]
    pl.semaphore_wait(barrier, len(partners))
    out = {}
    for g in range(kv_heads):
        for d in far:
            out[g, d] = send(
                kv.at[0, g], kv.at[d, g], fo_send.at[g, d], fo_recv.at[g, d], ahead(d)
            )

    off = offs[0]
    owner = lax.rem(me - off + n_dp, n_dp)
    chosen_len = plen[owner]
    row_at = lax.broadcasted_iota(jnp.int32, (PAIR * rows, rows), 0)
    row_at = jnp.where(row_at >= rows, row_at - rows, row_at)
    key_at = lax.broadcasted_iota(jnp.int32, (PAIR * rows, rows), 1)
    causal = row_at >= key_at
    valid = jnp.where(row_at[:, :1] < rlen[0], 1.0, 0.0)
    factor = valid * adv[0].astype(jnp.float32)
    prefix_ok = lax.broadcasted_iota(jnp.int32, (PAIR * rows, prefix_rows), 1) < chosen_len

    def head_cols(ref, p):
        return jnp.concatenate(
            [ref[:, (p * PAIR + u) * HD:(p * PAIR + u + 1) * HD] for u in range(PAIR)], axis=0
        )

    def put_cols(ref, p, value):
        for u in range(PAIR):
            ref[:, (p * PAIR + u) * HD:(p * PAIR + u + 1) * HD] = value[u * rows:(u + 1) * rows]

    def cols(g):
        return slice(g * HD, (g + 1) * HD)

    for name in ("okv", "q", "cot"):
        loads[name].wait()
    for p in range(pairs):
        g = p // group_pairs
        s = dot_nt(head_cols(q, p), okv[0, :, cols(g)]) * scale
        s = jnp.where(causal, s, MASKED_SCORE)
        m = jnp.max(s, axis=1, keepdims=True)
        e = jnp.exp(s - m)
        grad = (head_cols(cot, p).astype(jnp.float32) * factor).astype(jnp.bfloat16)
        gp = dot_nt(grad, okv[1, :, cols(g)])
        gs[p] = grad
        e_own[p] = e
        gp_own[p] = gp
        m_own[p] = m
        l_own[p] = jnp.sum(e, axis=1, keepdims=True)
        d_own[p] = jnp.sum(e * gp, axis=1, keepdims=True)

    back = {}
    part_rows = prefix_rows // PARTS

    def send_back(g, part):
        for d in far:
            back[g, part, d] = send(
                tx.at[d, part, g], rx.at[d, part, g],
                fi_send.at[d, part, g], fi_recv.at[d, part, g], behind(d),
            )

    for g in range(kv_heads):
        for d in far:
            out[g, d].wait_recv()
        keys, values = [
            sum(
                kv[d, g, i].astype(jnp.float32) * jnp.where(off == d, 1.0, 0.0)
                for d in range(window)
            ).astype(jnp.bfloat16)
            for i in range(2)
        ]
        chosen[g, 0] = keys
        chosen[g, 1] = values
        mine_pairs = range(g * group_pairs, (g + 1) * group_pairs)
        for p in mine_pairs:
            s = dot_nt(head_cols(q, p), keys) * scale
            s = jnp.where(prefix_ok, s, MASKED_SCORE)
            m = jnp.maximum(jnp.max(s, axis=1, keepdims=True), m_own[p])
            e = jnp.exp(s - m)
            a = jnp.exp(m_own[p] - m)
            r = 1.0 / (a * l_own[p] + jnp.sum(e, axis=1, keepdims=True))
            probs = e * r
            gp = dot_nt(gs[p], values)
            a = a * r
            delta = jnp.sum(probs * gp, axis=1, keepdims=True) + a * d_own[p]
            p_pre[p] = probs.astype(jnp.bfloat16)
            ds_pre[p] = (probs * (gp - delta)).astype(jnp.bfloat16)
            ratio[p] = a
            delta_s[p] = delta
        q_all = jnp.concatenate([head_cols(q, p) for p in mine_pairs], axis=0)
        ds_all = jnp.concatenate([ds_pre[p] for p in mine_pairs], axis=0)
        p_all = jnp.concatenate([p_pre[p] for p in mine_pairs], axis=0)
        g_all = jnp.concatenate([gs[p] for p in mine_pairs], axis=0)
        both = [dot_tn(ds_all, q_all) * scale, dot_tn(p_all, g_all)]
        for i in range(2):
            for d in range(window):
                share = both[i] * jnp.where(off == d, 1.0, 0.0)
                for part in range(PARTS):
                    piece = share[part * part_rows:(part + 1) * part_rows]
                    if d == 0:
                        mine[part, g, i] = piece
                    else:
                        tx[d, part, g, i] = piece.astype(jnp.bfloat16)
        send_back(g, 0)
    for part in range(1, PARTS):
        for g in range(kv_heads):
            send_back(g, part)

    stores = []

    def store(src, dst):
        copy = pltpu.make_async_copy(src, dst, out_sem.at[len(stores)])
        copy.start()
        stores.append(copy)

    def rest(g):
        mine_pairs = range(g * group_pairs, (g + 1) * group_pairs)
        keys = jnp.concatenate([chosen[g, 0], okv[0, :, cols(g)]], axis=0)
        values = jnp.concatenate([chosen[g, 1], okv[1, :, cols(g)]], axis=0)
        for p in mine_pairs:
            probs = e_own[p] * ratio[p]
            ds = (probs * (gp_own[p] - delta_s[p])).astype(jnp.bfloat16)
            probs = probs.astype(jnp.bfloat16)
            p_own[p] = probs
            ds_own[p] = ds
            out = dot_nn(jnp.concatenate([p_pre[p], probs], axis=1), values) * valid
            put_cols(attn, p, out.astype(jnp.bfloat16))
            grad = dot_nn(jnp.concatenate([ds_pre[p], ds], axis=1), keys) * scale
            put_cols(gq, p, grad.astype(jnp.bfloat16))
        q_all = jnp.concatenate([head_cols(q, p) for p in mine_pairs], axis=0)
        ds_all = jnp.concatenate([ds_own[p] for p in mine_pairs], axis=0)
        p_all = jnp.concatenate([p_own[p] for p in mine_pairs], axis=0)
        g_all = jnp.concatenate([gs[p] for p in mine_pairs], axis=0)
        gkv[0, :, cols(g)] = (dot_tn(ds_all, q_all) * scale).astype(jnp.bfloat16)
        gkv[1, :, cols(g)] = dot_tn(p_all, g_all).astype(jnp.bfloat16)

    for g in range(kv_heads):
        rest(g)
    store(attn, attn_hbm)
    store(gq, gq_hbm)
    store(gkv, gkv_hbm)

    block = depth // n_tensor
    chunk = block // COL_CHUNKS
    to_sibling = {}
    to_across = {}

    def project_back(part):
        grads = [[], []]
        for g in range(kv_heads):
            for d in far:
                back[g, part, d].wait_recv()
            for i in range(2):
                total = mine[part, g, i]
                for d in range(1, window):
                    total = total + rx[d, part, g, i].astype(jnp.float32)
                grads[i].append(total.astype(jnp.bfloat16))
        key_grad = jnp.concatenate(grads[0], axis=1)
        value_grad = jnp.concatenate(grads[1], axis=1)

        def partial(dx, to_core, c):
            at = (lax.rem(x_me + dx, n_x) * 2 + to_core) * block + c * chunk
            at = pl.ds(pl.multiple_of(at, chunk), chunk)
            return dot_nt(key_grad, wk[at, :]) + dot_nt(value_grad, wv[at, :])

        for dx in list(range(1, n_x)) + [0]:
            for c in range(COL_CHUNKS):
                sib_tx[part, dx, c] = partial(dx, 1 - core, c).astype(jnp.bfloat16)
                to_sibling[part, dx, c] = send(
                    sib_tx.at[part, dx, c], sib_rx.at[part, dx, c],
                    sib_send.at[part, dx, c], sib_recv.at[part, dx, c], (me, sibling),
                )
            for c in range(COL_CHUNKS):
                own = partial(dx, core, c)
                to_sibling[part, dx, c].wait_recv()
                own = own + sib_rx[part, dx, c].astype(jnp.float32)
                if dx == 0:
                    near[part, c] = own
                else:
                    x_tx[part, dx, c] = own.astype(jnp.bfloat16)
                    to_across[part, dx, c] = send(
                        x_tx.at[part, dx, c], x_rx.at[part, dx, c],
                        x_send.at[part, dx, c], x_recv.at[part, dx, c], across(dx),
                    )

    for part in range(PARTS):
        project_back(part)
    for part in range(PARTS):
        at = slice(part * part_rows, (part + 1) * part_rows)
        for c in range(COL_CHUNKS):
            own = near[part, c]
            for dx in range(1, n_x):
                to_across[part, dx, c].wait_recv()
                own = own + x_rx[part, dx, c].astype(jnp.float32)
            gph[at, c * chunk:(c + 1) * chunk] = own.astype(jnp.bfloat16)
    store(gph, gph_hbm)
    for group in (out, back, to_sibling, to_across):
        for copy in group.values():
            copy.wait_send()
    for copy in stores:
        copy.wait()


def hand_over(*refs):
    sources, targets, held, in_sem, out_sem = refs[:4], refs[4:8], refs[8:12], refs[12], refs[13]
    ins = [
        pltpu.make_async_copy(source, slot, in_sem.at[i])
        for i, (source, slot) in enumerate(zip(sources, held))
    ]
    outs = [
        pltpu.make_async_copy(slot, target, out_sem.at[i])
        for i, (slot, target) in enumerate(zip(held, targets))
    ]
    for copy in ins:
        copy.start()
    for came, goes in zip(ins, outs):
        came.wait()
        goes.start()
    for copy in outs:
        copy.wait()


def local(
    prompt_hidden, w_key, w_value, resp_query, resp_kv, cotangent,
    prompt_len, resp_len, offsets, advantage,
):
    n_dp, n_tensor = lax.axis_size("dp"), lax.axis_size("tensor")
    window = min(8, n_dp // 2)
    n_x = n_tensor // 2
    rows, width = resp_query.shape
    prefix_rows, depth = prompt_hidden.shape
    kv_width = w_key.shape[1]
    kv_heads = kv_width // HD
    pairs = width // HD // PAIR
    stacked = PAIR * rows
    block = depth // n_tensor
    chunk = block // COL_CHUNKS
    part_rows = prefix_rows // PARTS
    bf, f32 = jnp.bfloat16, jnp.float32
    vmem = pltpu.VMEM
    scratch = [
        vmem((prefix_rows, depth), bf),
        vmem((depth, kv_width), bf),
        vmem((depth, kv_width), bf),
        vmem((rows, width), bf),
        vmem((rows, width), bf),
        vmem((2, rows, kv_width), bf),
        vmem((window, kv_heads, 2, prefix_rows, HD), bf),
        vmem((kv_heads, 2, prefix_rows, HD), bf),
        vmem((pairs, stacked, rows), f32),
        vmem((pairs, stacked, rows), f32),
        vmem((pairs, stacked, HD), bf),
        vmem((pairs, stacked, 1), f32),
        vmem((pairs, stacked, 1), f32),
        vmem((pairs, stacked, 1), f32),
        vmem((pairs, stacked, prefix_rows), bf),
        vmem((pairs, stacked, prefix_rows), bf),
        vmem((pairs, stacked, rows), bf),
        vmem((pairs, stacked, rows), bf),
        vmem((pairs, stacked, 1), f32),
        vmem((pairs, stacked, 1), f32),
        vmem((window, PARTS, kv_heads, 2, part_rows, HD), bf),
        vmem((PARTS, kv_heads, 2, part_rows, HD), f32),
        vmem((window, PARTS, kv_heads, 2, part_rows, HD), bf),
        vmem((rows, width), bf),
        vmem((rows, width), bf),
        vmem((2, rows, kv_width), bf),
        vmem((prefix_rows, block), bf),
        vmem((PARTS, n_x, COL_CHUNKS, part_rows, chunk), bf),
        vmem((PARTS, n_x, COL_CHUNKS, part_rows, chunk), bf),
        vmem((PARTS, n_x, COL_CHUNKS, part_rows, chunk), bf),
        vmem((PARTS, n_x, COL_CHUNKS, part_rows, chunk), bf),
        vmem((PARTS, COL_CHUNKS, part_rows, chunk), f32),
        pltpu.SemaphoreType.DMA((3 * PROJ_CHUNKS + 3,)),
        pltpu.SemaphoreType.DMA((4,)),
        pltpu.SemaphoreType.DMA((kv_heads, window)),
        pltpu.SemaphoreType.DMA((kv_heads, window)),
        pltpu.SemaphoreType.DMA((window, PARTS, kv_heads)),
        pltpu.SemaphoreType.DMA((window, PARTS, kv_heads)),
        pltpu.SemaphoreType.DMA((PARTS, n_x, COL_CHUNKS)),
        pltpu.SemaphoreType.DMA((PARTS, n_x, COL_CHUNKS)),
        pltpu.SemaphoreType.DMA((PARTS, n_x, COL_CHUNKS)),
        pltpu.SemaphoreType.DMA((PARTS, n_x, COL_CHUNKS)),
    ]
    anywhere = pl.BlockSpec(memory_space=pl.ANY)
    scalars = pl.BlockSpec(memory_space=pltpu.SMEM)
    results = pl.pallas_call(
        functools.partial(kernel, n_dp, n_tensor, window),
        out_shape=(
            jax.ShapeDtypeStruct((rows, width), bf),
            jax.ShapeDtypeStruct((rows, width), bf),
            jax.ShapeDtypeStruct((2, rows, kv_width), bf),
            jax.ShapeDtypeStruct((prefix_rows, block), bf),
        ),
        in_specs=[anywhere] * 6 + [scalars] * 4,
        out_specs=(anywhere,) * 4,
        scratch_shapes=scratch,
        compiler_params=pltpu.CompilerParams(
            collective_id=0, has_side_effects=True, vmem_limit_bytes=56 * 2**20
        ),
    )(
        prompt_hidden, w_key, w_value, resp_query, resp_kv, cotangent,
        prompt_len, resp_len, offsets, advantage,
    )
    return pl.pallas_call(
        hand_over,
        out_shape=tuple(jax.ShapeDtypeStruct(a.shape, a.dtype) for a in results),
        in_specs=[anywhere] * 4,
        out_specs=(anywhere,) * 4,
        scratch_shapes=[vmem(a.shape, a.dtype) for a in results]
        + [pltpu.SemaphoreType.DMA((4,)), pltpu.SemaphoreType.DMA((4,))],
    )(*results)


def solution(mesh):
    placed = (
        P("dp", None),
        P(None, "tensor"),
        P(None, "tensor"),
        P("dp", "tensor"),
        P(None, "dp", "tensor"),
        P("dp", "tensor"),
        P(),
        P("dp"),
        P("dp"),
        P("dp"),
    )
    return jax.shard_map(
        local,
        mesh=mesh,
        in_specs=placed,
        out_specs=(
            P("dp", "tensor"),
            P("dp", "tensor"),
            P(None, "dp", "tensor"),
            P("dp", "tensor"),
        ),
        check_vma=False,
    )
```

```python
import functools

import jax
import jax.numpy as jnp
from jax import lax
from jax.experimental import pallas as pl
from jax.experimental.pallas import tpu as pltpu
from jax.sharding import PartitionSpec as P

HD = 128
MASKED_SCORE = -1e30
PAIR = 2
PROJ_CHUNKS = 4
COL_CHUNKS = 5
PARTS = 2
MESH = pl.DeviceIdType.MESH
NT = (((1,), (1,)), ((), ()))
TN = (((0,), (0,)), ((), ()))


def dot_nt(a, b):
    return lax.dot_general(a, b, NT, preferred_element_type=jnp.float32)


def dot_tn(a, b):
    return lax.dot_general(a, b, TN, preferred_element_type=jnp.float32)


def dot_nn(a, b):
    return jnp.dot(a, b, preferred_element_type=jnp.float32)


def kernel(
    n_dp, n_tensor, window,
    hid_hbm, wk_hbm, wv_hbm, q_hbm, okv_hbm, cot_hbm, plen_hbm, rlen_hbm, offs_hbm, adv_hbm,
    attn_hbm, gq_hbm, gkv_hbm, gph_hbm,
    plen, rlen, offs, adv, hid, wk, wv, q, cot, okv, kv, chosen, e_own, gp_own, gs, m_own, l_own, d_own,
    p_pre, ds_pre, p_own, ds_own, ratio, delta_s,
    tx, mine, rx, attn, gq, gkv, gph, sib_tx, sib_rx, x_tx, x_rx, near,
    in_sem, out_sem, fo_send, fo_recv, fi_send, fi_recv, sib_send, sib_recv, x_send, x_recv,
):
    me = lax.axis_index("dp")
    t_me = lax.axis_index("tensor")
    n_x = n_tensor // 2
    x_me, core = lax.div(t_me, 2), lax.rem(t_me, 2)
    sibling = x_me * 2 + 1 - core
    rows, width = q.shape
    prefix_rows, depth = hid.shape
    kv_width = wk.shape[1]
    kv_heads = kv_width // HD
    pairs = width // HD // PAIR
    group_pairs = pairs // kv_heads
    scale = HD ** (-0.5)
    far = range(window - 1, 0, -1)

    def ahead(d):
        return (lax.rem(me + d, n_dp), t_me)

    def behind(d):
        return (lax.rem(me + n_dp - d, n_dp), t_me)

    def across(dx):
        return (me, lax.rem(x_me + dx, n_x) * 2 + core)

    barrier = pltpu.get_barrier_semaphore()
    partners = [ahead(d) for d in far] + [behind(d) for d in far]
    partners += [(me, sibling)] + [across(dx) for dx in range(1, n_x)]
    for partner in partners:
        pl.semaphore_signal(barrier, inc=1, device_id=partner, device_id_type=MESH)

    step = depth // PROJ_CHUNKS
    loads = {}

    def load(name, src, dst):
        copy = pltpu.make_async_copy(src, dst, in_sem.at[len(loads)])
        copy.start()
        loads[name] = copy

    for c in range(PROJ_CHUNKS):
        part = pl.ds(c * step, step)
        load(("h", c), hid_hbm.at[:, part], hid.at[:, part])
        load(("k", c), wk_hbm.at[part, :], wk.at[part, :])
    for c in range(PROJ_CHUNKS):
        part = pl.ds(c * step, step)
        load(("v", c), wv_hbm.at[part, :], wv.at[part, :])
    load("okv", okv_hbm, okv)
    load("q", q_hbm, q)
    load("cot", cot_hbm, cot)
    small = {"plen": (plen_hbm, plen), "rlen": (rlen_hbm, rlen), "offs": (offs_hbm, offs)}
    small["adv"] = (adv_hbm, adv)
    for name in small:
        load(name, *small[name])

    def projected(name, weight):
        total = None
        for c in range(PROJ_CHUNKS):
            if name == "k":
                loads[("h", c)].wait()
            loads[(name, c)].wait()
            part = pl.ds(c * step, step)
            term = dot_nn(hid[:, part], weight[part, :])
            total = term if total is None else total + term
        return total.astype(jnp.bfloat16)

    def send(src, dst, send_sem, recv_sem, device):
        copy = pltpu.make_async_remote_copy(
            src_ref=src, dst_ref=dst, send_sem=send_sem, recv_sem=recv_sem,
            device_id=device, device_id_type=MESH,
        )
        copy.start()
        return copy

    for i, (name, weight) in enumerate((("k", wk), ("v", wv))):
        block = projected(name, weight)
        for g in range(kv_heads):
            kv[0, g, i] = block[:, g * HD:(g + 1) * HD]
    pl.semaphore_wait(barrier, len(partners))
    out = {}
    for g in range(kv_heads):
        for d in far:
            out[g, d] = send(
                kv.at[0, g], kv.at[d, g], fo_send.at[g, d], fo_recv.at[g, d], ahead(d)
            )

    for name in small:
        loads[name].wait()
    off = offs[0]
    owner = lax.rem(me - off + n_dp, n_dp)
    chosen_len = plen[owner]
    row_at = lax.broadcasted_iota(jnp.int32, (PAIR * rows, rows), 0)
    row_at = jnp.where(row_at >= rows, row_at - rows, row_at)
    key_at = lax.broadcasted_iota(jnp.int32, (PAIR * rows, rows), 1)
    causal = row_at >= key_at
    valid = jnp.where(row_at[:, :1] < rlen[0], 1.0, 0.0)
    factor = valid * adv[0].astype(jnp.float32)
    prefix_ok = lax.broadcasted_iota(jnp.int32, (PAIR * rows, prefix_rows), 1) < chosen_len

    def head_cols(ref, p):
        return jnp.concatenate(
            [ref[:, (p * PAIR + u) * HD:(p * PAIR + u + 1) * HD] for u in range(PAIR)], axis=0
        )

    def put_cols(ref, p, value):
        for u in range(PAIR):
            ref[:, (p * PAIR + u) * HD:(p * PAIR + u + 1) * HD] = value[u * rows:(u + 1) * rows]

    def cols(g):
        return slice(g * HD, (g + 1) * HD)

    for name in ("okv", "q", "cot"):
        loads[name].wait()
    for p in range(pairs):
        g = p // group_pairs
        s = dot_nt(head_cols(q, p), okv[0, :, cols(g)]) * scale
        s = jnp.where(causal, s, MASKED_SCORE)
        m = jnp.max(s, axis=1, keepdims=True)
        e = jnp.exp(s - m)
        grad = (head_cols(cot, p).astype(jnp.float32) * factor).astype(jnp.bfloat16)
        gp = dot_nt(grad, okv[1, :, cols(g)])
        gs[p] = grad
        e_own[p] = e
        gp_own[p] = gp
        m_own[p] = m
        l_own[p] = jnp.sum(e, axis=1, keepdims=True)
        d_own[p] = jnp.sum(e * gp, axis=1, keepdims=True)

    back = {}
    part_rows = prefix_rows // PARTS

    def send_back(g, part):
        for d in far:
            back[g, part, d] = send(
                tx.at[d, part, g], rx.at[d, part, g],
                fi_send.at[d, part, g], fi_recv.at[d, part, g], behind(d),
            )

    for g in range(kv_heads):
        for d in far:
            out[g, d].wait_recv()
        keys, values = [
            sum(
                kv[d, g, i].astype(jnp.float32) * jnp.where(off == d, 1.0, 0.0)
                for d in range(window)
            ).astype(jnp.bfloat16)
            for i in range(2)
        ]
        chosen[g, 0] = keys
        chosen[g, 1] = values
        mine_pairs = range(g * group_pairs, (g + 1) * group_pairs)
        for p in mine_pairs:
            s = dot_nt(head_cols(q, p), keys) * scale
            s = jnp.where(prefix_ok, s, MASKED_SCORE)
            m = jnp.maximum(jnp.max(s, axis=1, keepdims=True), m_own[p])
            e = jnp.exp(s - m)
            a = jnp.exp(m_own[p] - m)
            r = 1.0 / (a * l_own[p] + jnp.sum(e, axis=1, keepdims=True))
            probs = e * r
            gp = dot_nt(gs[p], values)
            a = a * r
            delta = jnp.sum(probs * gp, axis=1, keepdims=True) + a * d_own[p]
            p_pre[p] = probs.astype(jnp.bfloat16)
            ds_pre[p] = (probs * (gp - delta)).astype(jnp.bfloat16)
            ratio[p] = a
            delta_s[p] = delta
        q_all = jnp.concatenate([head_cols(q, p) for p in mine_pairs], axis=0)
        ds_all = jnp.concatenate([ds_pre[p] for p in mine_pairs], axis=0)
        p_all = jnp.concatenate([p_pre[p] for p in mine_pairs], axis=0)
        g_all = jnp.concatenate([gs[p] for p in mine_pairs], axis=0)
        both = [dot_tn(ds_all, q_all) * scale, dot_tn(p_all, g_all)]
        for i in range(2):
            for d in range(window):
                share = both[i] * jnp.where(off == d, 1.0, 0.0)
                for part in range(PARTS):
                    piece = share[part * part_rows:(part + 1) * part_rows]
                    if d == 0:
                        mine[part, g, i] = piece
                    else:
                        tx[d, part, g, i] = piece.astype(jnp.bfloat16)
        send_back(g, 0)
    for part in range(1, PARTS):
        for g in range(kv_heads):
            send_back(g, part)

    stores = []

    def store(src, dst):
        copy = pltpu.make_async_copy(src, dst, out_sem.at[len(stores)])
        copy.start()
        stores.append(copy)

    def rest(g):
        mine_pairs = range(g * group_pairs, (g + 1) * group_pairs)
        keys = jnp.concatenate([chosen[g, 0], okv[0, :, cols(g)]], axis=0)
        values = jnp.concatenate([chosen[g, 1], okv[1, :, cols(g)]], axis=0)
        for p in mine_pairs:
            probs = e_own[p] * ratio[p]
            ds = (probs * (gp_own[p] - delta_s[p])).astype(jnp.bfloat16)
            probs = probs.astype(jnp.bfloat16)
            p_own[p] = probs
            ds_own[p] = ds
            out = dot_nn(jnp.concatenate([p_pre[p], probs], axis=1), values) * valid
            put_cols(attn, p, out.astype(jnp.bfloat16))
            grad = dot_nn(jnp.concatenate([ds_pre[p], ds], axis=1), keys) * scale
            put_cols(gq, p, grad.astype(jnp.bfloat16))
        q_all = jnp.concatenate([head_cols(q, p) for p in mine_pairs], axis=0)
        ds_all = jnp.concatenate([ds_own[p] for p in mine_pairs], axis=0)
        p_all = jnp.concatenate([p_own[p] for p in mine_pairs], axis=0)
        g_all = jnp.concatenate([gs[p] for p in mine_pairs], axis=0)
        gkv[0, :, cols(g)] = (dot_tn(ds_all, q_all) * scale).astype(jnp.bfloat16)
        gkv[1, :, cols(g)] = dot_tn(p_all, g_all).astype(jnp.bfloat16)

    for g in range(kv_heads):
        rest(g)
    store(attn, attn_hbm)
    store(gq, gq_hbm)
    store(gkv, gkv_hbm)

    block = depth // n_tensor
    chunk = block // COL_CHUNKS
    to_sibling = {}
    to_across = {}

    def project_back(part):
        grads = [[], []]
        for g in range(kv_heads):
            for d in far:
                back[g, part, d].wait_recv()
            for i in range(2):
                total = mine[part, g, i]
                for d in range(1, window):
                    total = total + rx[d, part, g, i].astype(jnp.float32)
                grads[i].append(total.astype(jnp.bfloat16))
        key_grad = jnp.concatenate(grads[0], axis=1)
        value_grad = jnp.concatenate(grads[1], axis=1)

        def partial(dx, to_core, c):
            at = (lax.rem(x_me + dx, n_x) * 2 + to_core) * block + c * chunk
            at = pl.ds(pl.multiple_of(at, chunk), chunk)
            return dot_nt(key_grad, wk[at, :]) + dot_nt(value_grad, wv[at, :])

        for dx in list(range(1, n_x)) + [0]:
            for c in range(COL_CHUNKS):
                sib_tx[part, dx, c] = partial(dx, 1 - core, c).astype(jnp.bfloat16)
                to_sibling[part, dx, c] = send(
                    sib_tx.at[part, dx, c], sib_rx.at[part, dx, c],
                    sib_send.at[part, dx, c], sib_recv.at[part, dx, c], (me, sibling),
                )
            for c in range(COL_CHUNKS):
                own = partial(dx, core, c)
                to_sibling[part, dx, c].wait_recv()
                own = own + sib_rx[part, dx, c].astype(jnp.float32)
                if dx == 0:
                    near[part, c] = own
                else:
                    x_tx[part, dx, c] = own.astype(jnp.bfloat16)
                    to_across[part, dx, c] = send(
                        x_tx.at[part, dx, c], x_rx.at[part, dx, c],
                        x_send.at[part, dx, c], x_recv.at[part, dx, c], across(dx),
                    )

    for part in range(PARTS):
        project_back(part)
    for part in range(PARTS):
        at = slice(part * part_rows, (part + 1) * part_rows)
        for c in range(COL_CHUNKS):
            own = near[part, c]
            for dx in range(1, n_x):
                to_across[part, dx, c].wait_recv()
                own = own + x_rx[part, dx, c].astype(jnp.float32)
            gph[at, c * chunk:(c + 1) * chunk] = own.astype(jnp.bfloat16)
    store(gph, gph_hbm)
    for group in (out, back, to_sibling, to_across):
        for copy in group.values():
            copy.wait_send()
    for copy in stores:
        copy.wait()


def hand_over(*refs):
    sources, targets, held, in_sem, out_sem = refs[:4], refs[4:8], refs[8:12], refs[12], refs[13]
    ins = [
        pltpu.make_async_copy(source, slot, in_sem.at[i])
        for i, (source, slot) in enumerate(zip(sources, held))
    ]
    outs = [
        pltpu.make_async_copy(slot, target, out_sem.at[i])
        for i, (slot, target) in enumerate(zip(held, targets))
    ]
    for copy in ins:
        copy.start()
    for came, goes in zip(ins, outs):
        came.wait()
        goes.start()
    for copy in outs:
        copy.wait()


def local(
    prompt_hidden, w_key, w_value, resp_query, resp_kv, cotangent,
    prompt_len, resp_len, offsets, advantage,
):
    n_dp, n_tensor = lax.axis_size("dp"), lax.axis_size("tensor")
    window = min(8, n_dp // 2)
    n_x = n_tensor // 2
    rows, width = resp_query.shape
    prefix_rows, depth = prompt_hidden.shape
    kv_width = w_key.shape[1]
    kv_heads = kv_width // HD
    pairs = width // HD // PAIR
    stacked = PAIR * rows
    block = depth // n_tensor
    chunk = block // COL_CHUNKS
    part_rows = prefix_rows // PARTS
    bf, f32 = jnp.bfloat16, jnp.float32
    vmem = pltpu.VMEM
    scratch = [pltpu.SMEM(a.shape, a.dtype) for a in (prompt_len, resp_len, offsets, advantage)]
    scratch += [
        vmem((prefix_rows, depth), bf),
        vmem((depth, kv_width), bf),
        vmem((depth, kv_width), bf),
        vmem((rows, width), bf),
        vmem((rows, width), bf),
        vmem((2, rows, kv_width), bf),
        vmem((window, kv_heads, 2, prefix_rows, HD), bf),
        vmem((kv_heads, 2, prefix_rows, HD), bf),
        vmem((pairs, stacked, rows), f32),
        vmem((pairs, stacked, rows), f32),
        vmem((pairs, stacked, HD), bf),
        vmem((pairs, stacked, 1), f32),
        vmem((pairs, stacked, 1), f32),
        vmem((pairs, stacked, 1), f32),
        vmem((pairs, stacked, prefix_rows), bf),
        vmem((pairs, stacked, prefix_rows), bf),
        vmem((pairs, stacked, rows), bf),
        vmem((pairs, stacked, rows), bf),
        vmem((pairs, stacked, 1), f32),
        vmem((pairs, stacked, 1), f32),
        vmem((window, PARTS, kv_heads, 2, part_rows, HD), bf),
        vmem((PARTS, kv_heads, 2, part_rows, HD), f32),
        vmem((window, PARTS, kv_heads, 2, part_rows, HD), bf),
        vmem((rows, width), bf),
        vmem((rows, width), bf),
        vmem((2, rows, kv_width), bf),
        vmem((prefix_rows, block), bf),
        vmem((PARTS, n_x, COL_CHUNKS, part_rows, chunk), bf),
        vmem((PARTS, n_x, COL_CHUNKS, part_rows, chunk), bf),
        vmem((PARTS, n_x, COL_CHUNKS, part_rows, chunk), bf),
        vmem((PARTS, n_x, COL_CHUNKS, part_rows, chunk), bf),
        vmem((PARTS, COL_CHUNKS, part_rows, chunk), f32),
        pltpu.SemaphoreType.DMA((3 * PROJ_CHUNKS + 7,)),
        pltpu.SemaphoreType.DMA((4,)),
        pltpu.SemaphoreType.DMA((kv_heads, window)),
        pltpu.SemaphoreType.DMA((kv_heads, window)),
        pltpu.SemaphoreType.DMA((window, PARTS, kv_heads)),
        pltpu.SemaphoreType.DMA((window, PARTS, kv_heads)),
        pltpu.SemaphoreType.DMA((PARTS, n_x, COL_CHUNKS)),
        pltpu.SemaphoreType.DMA((PARTS, n_x, COL_CHUNKS)),
        pltpu.SemaphoreType.DMA((PARTS, n_x, COL_CHUNKS)),
        pltpu.SemaphoreType.DMA((PARTS, n_x, COL_CHUNKS)),
    ]
    anywhere = pl.BlockSpec(memory_space=pl.ANY)
    results = pl.pallas_call(
        functools.partial(kernel, n_dp, n_tensor, window),
        out_shape=(
            jax.ShapeDtypeStruct((rows, width), bf),
            jax.ShapeDtypeStruct((rows, width), bf),
            jax.ShapeDtypeStruct((2, rows, kv_width), bf),
            jax.ShapeDtypeStruct((prefix_rows, block), bf),
        ),
        in_specs=[anywhere] * 10,
        out_specs=(anywhere,) * 4,
        scratch_shapes=scratch,
        compiler_params=pltpu.CompilerParams(
            collective_id=0, has_side_effects=True, vmem_limit_bytes=56 * 2**20
        ),
    )(
        prompt_hidden, w_key, w_value, resp_query, resp_kv, cotangent,
        prompt_len, resp_len, offsets, advantage,
    )
    return pl.pallas_call(
        hand_over,
        out_shape=tuple(jax.ShapeDtypeStruct(a.shape, a.dtype) for a in results),
        in_specs=[anywhere] * 4,
        out_specs=(anywhere,) * 4,
        scratch_shapes=[vmem(a.shape, a.dtype) for a in results]
        + [pltpu.SemaphoreType.DMA((4,)), pltpu.SemaphoreType.DMA((4,))],
    )(*results)


def solution(mesh):
    placed = (
        P("dp", None),
        P(None, "tensor"),
        P(None, "tensor"),
        P("dp", "tensor"),
        P(None, "dp", "tensor"),
        P("dp", "tensor"),
        P(),
        P("dp"),
        P("dp"),
        P("dp"),
    )
    return jax.shard_map(
        local,
        mesh=mesh,
        in_specs=placed,
        out_specs=(
            P("dp", "tensor"),
            P("dp", "tensor"),
            P(None, "dp", "tensor"),
            P("dp", "tensor"),
        ),
        check_vma=False,
    )
```
